256 devices in a mesh: layer: 16 (over z, x_hi), latent: 16 (over x_lo, y, core).
Axes of the slice: x: 4 (x_hi: 2, x_lo: 2; x = x_hi * 2 + x_lo), y: 4, z: 8, core: 2. Of those that a mesh axis runs over, the one named last changes fastest.
Arguments:
- activations: bfloat16 [16, 1024, 2048], P('layer', 'latent'), may hold values from -6 to 6
- cotangents: bfloat16 [16, 1024, 2048], P('layer', 'latent'), may hold values from -0.375 to 0.375
- enc_weight: bfloat16 [16, 2048, 8192], P('layer', None, 'latent'), may hold values from -0.03125 to 0.03125
- dec_weight: bfloat16 [16, 8192, 2048], P('layer', 'latent'), may hold values from -0.03125 to 0.03125
- enc_bias: float32 [8192], P('latent'), may hold values from -3 to 3
- active_mask: int32 [1024, 8192], P(None, 'latent'), may hold values from 0 to 1, as said below
Outputs:
- enc_grad: bfloat16 [16, 2048, 8192], P('layer', None, 'latent')
- dec_grad: bfloat16 [16, 8192, 2048], P('layer', 'latent')
- bias_grad: float32 [8192], P('latent')
The draws below stay inside these ranges and needn't reach their ends.
Inputs may be any that keep to these rules, and one draw needn't show every extreme that they name: `active_mask`: every token has exactly 64 ones among the 8192 latents.
All inputs are finite; a program needn't handle non-finite values.
Results may differ from the reference program's by a relative error of at most 0.007.
Values may be sent and summed in bfloat16 or wider, within the bound.
No kernel may reach another device: no remote copies, remote signals or barrier semaphores. Data moves between devices by JAX's collectives and lax.ppermute only.
A program may use at most 64 MiB of HBM per device.

```python
import jax
import jax.numpy as jnp
from jax import lax

D = 2048
TOPK = 64
LAYERS = 16
LATENTS = 8192
TOKENS = 1024


def draw_active_mask(key, part):
    key = jax.random.fold_in(key, 11)
    row_keys = jax.random.split(key, TOKENS)
    orders = jax.vmap(lambda row_key: jax.random.permutation(row_key, LATENTS))(row_keys)
    chosen = orders[:, :TOPK].astype(jnp.int32)
    rows = jnp.broadcast_to(jnp.arange(TOKENS, dtype=jnp.int32)[:, None], (TOKENS, TOPK))
    return jnp.zeros((TOKENS, LATENTS), jnp.int32).at[rows, chosen].set(1)


def block_scale(key, shape, shards, low, largest):
    level = 1.0
    for position, blocks in shards:
        draws = jax.random.uniform(jax.random.fold_in(jax.random.fold_in(key, 6), position), (blocks,), jnp.float32, low / len(shards), largest / len(shards))
        level = level * jnp.repeat(jnp.exp(draws), shape[position] // blocks).reshape((-1,) + (1,) * (len(shape) - 1 - position))
    return level


def noise(stream_key, dims, spread, reach, pieces=(), kind=jnp.bfloat16):
    values = jax.random.normal(stream_key, dims, jnp.float32) * spread
    if len(pieces) > 0:
        values = block_scale(stream_key, dims, pieces, -0.22, 0.18) * values
    return jnp.clip(values, min=-reach, max=reach).astype(kind)


def setup_inputs(seed: int = 0) -> dict:
    splits = jax.random.split(jax.random.key(seed), 7)
    return {
        "activations": noise(splits[0], (LAYERS, TOKENS, D), 1.0, 6.0, ((0, 16), (1, 16))),
        "cotangents": noise(splits[1], (LAYERS, TOKENS, D), 0.0625, 0.375, ((0, 16), (1, 16))),
        "enc_weight": noise(splits[2], (LAYERS, D, LATENTS), (D * LAYERS) ** -0.5, 0.03125, ((0, 16), (2, 16))),
        "dec_weight": noise(splits[3], (LAYERS, LATENTS, D), (D * LAYERS) ** -0.5, 0.03125, ((0, 16), (1, 16))),
        "enc_bias": noise(splits[4], (LATENTS,), 0.5, 3.0, ((0, 16),), jnp.float32),
        "active_mask": draw_active_mask(jax.random.fold_in(splits[6], 71), 0),
    }


def reference(activations, cotangents, enc_weight, dec_weight, enc_bias, active_mask):
    mask_float = active_mask.astype(jnp.float32)
    preact = jnp.zeros((TOKENS, LATENTS), jnp.float32)
    code_cot = jnp.zeros((TOKENS, LATENTS), jnp.float32)
    for layer_index in range(LAYERS):
        preact = preact + jnp.dot(activations[layer_index], enc_weight[layer_index], preferred_element_type=jnp.float32)
        code_cot = code_cot + lax.dot_general(cotangents[layer_index], dec_weight[layer_index], (((1,), (1,)), ((), ())), preferred_element_type=jnp.float32)
    preact = preact + enc_bias[None, :]
    code = (mask_float * preact).astype(jnp.bfloat16)
    pre_cot = (mask_float * code_cot).astype(jnp.bfloat16)
    enc_list = []
    dec_list = []
    for layer_index in range(LAYERS):
        dec_list.append(lax.dot_general(code, cotangents[layer_index], (((0,), (0,)), ((), ())), preferred_element_type=jnp.float32).astype(jnp.bfloat16))
        enc_list.append(lax.dot_general(activations[layer_index], pre_cot, (((0,), (0,)), ((), ())), preferred_element_type=jnp.float32).astype(jnp.bfloat16))
    bias_grad = jnp.sum(pre_cot.astype(jnp.float32), axis=0)
    return jnp.stack(enc_list), jnp.stack(dec_list), bias_grad
```

```python
import jax
import jax.numpy as jnp
from jax import lax
from jax.experimental import pallas as pl
from jax.experimental.pallas import tpu as pltpu
from jax.sharding import PartitionSpec as P

KEEP = 64
VMEM = 56 * 1024 * 1024


def take(values, lanes):
    return jnp.take_along_axis(values, lanes, axis=1, mode="promise_in_bounds")


def tiles_of(array):
    return [array[:, at : at + 128] for at in range(0, array.shape[1], 128)]


def rank_kernel(mask_ref, rank_ref, slot_ref):
    mask = mask_ref[...]
    rows, latents = mask.shape
    half = rows // 2
    shape = (latents, latents)
    upper = lax.broadcasted_iota(jnp.int32, shape, 0) <= lax.broadcasted_iota(jnp.int32, shape, 1)
    upper = upper.astype(jnp.float32).astype(jnp.bfloat16)
    ones = mask.astype(jnp.float32).astype(jnp.bfloat16)
    count = jnp.dot(ones, upper, preferred_element_type=jnp.float32).astype(jnp.int32)
    rank_ref[...] = jnp.where(mask > 0, count - 1, -1)
    tiles = tiles_of(count)
    lane = lax.broadcasted_iota(jnp.int32, (rows, 128), 1)
    place = lane % KEEP
    tile = jnp.zeros((rows, 128), jnp.int32)
    for part in tiles[:-1]:
        tile += jnp.where(take(part, jnp.full((rows, 128), 127, jnp.int32)) <= place, 1, 0)
    at = jnp.zeros((rows, 128), jnp.int32)
    for step in (64, 32, 16, 8, 4, 2, 1):
        probe = at + (step - 1)
        seen = take(tiles[0], probe)
        for number in range(1, len(tiles)):
            seen = jnp.where(tile == number, take(tiles[number], probe), seen)
        at += jnp.where(seen <= place, step, 0)
    slot = tile * 128 + at
    slot_ref[...] = jnp.where(lane[:half] < KEEP, slot[:half], slot[half:])


def squeeze(full, slot):
    half = slot.shape[0]
    lane = lax.broadcasted_iota(jnp.int32, (half, 128), 1)
    tile, at = slot // 128, slot % 128
    out = jnp.zeros((half, 128), jnp.float32)
    for number, part in enumerate(tiles_of(full)):
        got = jnp.where(lane < KEEP, take(part[:half], at), take(part[half:], at))
        out = jnp.where(tile == number, got, out)
    return out


def spread(packed, rank):
    half = packed.shape[0]
    parts = []
    for number, place in enumerate(tiles_of(rank)):
        at = jnp.maximum(place, 0)
        got = jnp.concatenate([take(packed, at[:half]), take(packed, at[half:] + KEEP)], axis=0)
        parts.append(jnp.where(place >= 0, got, 0.0))
    return jnp.concatenate(parts, axis=1)


def term_kernel(acts_ref, cots_ref, enc_ref, dec_ref, slot_ref, out_ref):
    blocks, _, rows, width = acts_ref.shape
    half = rows // 2
    acts = acts_ref[...].reshape(blocks * rows, width)
    pre = jnp.dot(acts, enc_ref[...], preferred_element_type=jnp.float32)
    cots = cots_ref[...].reshape(blocks * rows, width)
    cot = lax.dot_general(cots, dec_ref[...], (((1,), (1,)), ((), ())), preferred_element_type=jnp.float32)
    for block in range(blocks):
        slot = slot_ref[block * half : (block + 1) * half, :]
        at = slice(block * rows, (block + 1) * rows)
        out_ref[block, :half] = squeeze(pre[at], slot).astype(out_ref.dtype)
        out_ref[block, half:] = squeeze(cot[at], slot).astype(out_ref.dtype)


def sum_kernel(place_ref, terms_ref, slot_ref, bias_ref, out_ref):
    total = jnp.sum(terms_ref[...].astype(jnp.float32), axis=0)
    half = slot_ref.shape[0]
    bias = jnp.broadcast_to(bias_ref[...], (2 * half, bias_ref.shape[1]))
    code = total[:half] + squeeze(bias, slot_ref[...])
    both = jnp.concatenate([code, total[half:]], axis=0).astype(out_ref.dtype)
    out_ref[...] = jnp.broadcast_to(both[None], out_ref.shape)


def grad_kernel(sums_ref, rank_ref, acts_ref, cots_ref, enc_ref, dec_ref, bias_ref, code_ref, pre_ref):
    blocks, pair, _ = sums_ref.shape
    half = pair // 2
    tokens = rank_ref.shape[0]

    @pl.when(pl.program_id(0) == 0)
    def _():
        total = jnp.zeros(bias_ref.shape, jnp.float32)
        for block in range(blocks):
            at = slice(block * pair, (block + 1) * pair)
            rank = rank_ref[at, :]
            packed = sums_ref[block].astype(jnp.float32)
            code_ref[at, :] = spread(packed[:half], rank).astype(code_ref.dtype)
            pre = spread(packed[half:], rank)
            pre_ref[at, :] = pre.astype(pre_ref.dtype)
            total += jnp.sum(pre, axis=0, keepdims=True)
        bias_ref[...] = total

    over_tokens = (((0,), (0,)), ((), ()))
    cots = cots_ref[...].reshape(tokens, -1)
    dec = lax.dot_general(code_ref[...], cots, over_tokens, preferred_element_type=jnp.float32)
    dec_ref[...] = dec.astype(dec_ref.dtype)
    acts = acts_ref[...].reshape(tokens, -1)
    enc = lax.dot_general(acts, pre_ref[...], over_tokens, preferred_element_type=jnp.float32)
    enc_ref[...] = enc.astype(enc_ref.dtype)


def params():
    return pltpu.CompilerParams(vmem_limit_bytes=VMEM)


def local(activations, cotangents, enc_weight, dec_weight, enc_bias, active_mask):
    tokens, latents = active_mask.shape
    rows, width = activations.shape[1:]
    blocks = tokens // rows
    half = rows // 2
    layers = blocks
    f32, bf16 = jnp.float32, jnp.bfloat16

    own = jnp.stack([activations[0], cotangents[0]])
    both = lax.all_gather(own, "latent", axis=0, tiled=False)

    rank, slot = pl.pallas_call(
        rank_kernel,
        grid=(blocks,),
        in_specs=[pl.BlockSpec((rows, latents), lambda i: (i, 0))],
        out_specs=[pl.BlockSpec((rows, latents), lambda i: (i, 0)), pl.BlockSpec((half, 128), lambda i: (i, 0))],
        out_shape=[
            jax.ShapeDtypeStruct((tokens, latents), jnp.int32),
            jax.ShapeDtypeStruct((tokens // 2, 128), jnp.int32),
        ],
        compiler_params=params(),
        cost_estimate=pl.CostEstimate(flops=8 * 10**9, bytes_accessed=5 * 10**6, transcendentals=0),
        name="ranks",
    )(active_mask)

    group = 4
    terms = pl.pallas_call(
        term_kernel,
        grid=(blocks // group,),
        in_specs=[
            pl.BlockSpec((group, 1, rows, width), lambda i: (i, 0, 0, 0)),
            pl.BlockSpec((group, 1, rows, width), lambda i: (i, 1, 0, 0)),
            pl.BlockSpec((width, latents), lambda i: (0, 0)),
            pl.BlockSpec((latents, width), lambda i: (0, 0)),
            pl.BlockSpec((group * half, 128), lambda i: (i, 0)),
        ],
        out_specs=pl.BlockSpec((group, 2 * half, 128), lambda i: (i, 0, 0)),
        out_shape=jax.ShapeDtypeStruct((blocks, 2 * half, 128), bf16),
        compiler_params=params(),
        name="terms",
    )(both, both, enc_weight[0], dec_weight[0], slot)

    mine = lax.all_to_all(terms, "layer", 0, 0)
    place = lax.axis_index("layer").astype(jnp.int32)[None]
    sums = pl.pallas_call(
        sum_kernel,
        grid_spec=pltpu.PrefetchScalarGridSpec(
            num_scalar_prefetch=1,
            grid=(1,),
            in_specs=[
                pl.BlockSpec((layers, 2 * half, 128), lambda i, place: (0, 0, 0)),
                pl.BlockSpec((half, 128), lambda i, place: (place[0], 0)),
                pl.BlockSpec((1, latents), lambda i, place: (0, 0)),
            ],
            out_specs=pl.BlockSpec((layers, 2 * half, 128), lambda i, place: (0, 0, 0)),
        ),
        out_shape=jax.ShapeDtypeStruct((layers, 2 * half, 128), bf16),
        compiler_params=params(),
        name="sums",
    )(place, mine, slot, enc_bias[None, :])
    sums = lax.all_to_all(sums, "layer", 0, 0)

    cut = 256
    enc_grad, dec_grad, bias_grad = pl.pallas_call(
        grad_kernel,
        grid=(width // cut,),
        in_specs=[
            pl.BlockSpec((blocks, 2 * half, 128), lambda i: (0, 0, 0)),
            pl.BlockSpec((tokens, latents), lambda i: (0, 0)),
            pl.BlockSpec((blocks, 1, rows, cut), lambda i: (0, 0, 0, i)),
            pl.BlockSpec((blocks, 1, rows, cut), lambda i: (0, 1, 0, i)),
        ],
        out_specs=[
            pl.BlockSpec((cut, latents), lambda i: (i, 0)),
            pl.BlockSpec((latents, cut), lambda i: (0, i)),
            pl.BlockSpec((1, latents), lambda i: (0, 0)),
        ],
        out_shape=[
            jax.ShapeDtypeStruct((width, latents), bf16),
            jax.ShapeDtypeStruct((latents, width), bf16),
            jax.ShapeDtypeStruct((1, latents), f32),
        ],
        scratch_shapes=[pltpu.VMEM((tokens, latents), bf16), pltpu.VMEM((tokens, latents), bf16)],
        compiler_params=params(),
        name="grads",
    )(sums, rank, both, both)
    return enc_grad[None], dec_grad[None], bias_grad[0]


def solution(mesh):
    return jax.shard_map(
        local,
        mesh=mesh,
        in_specs=(
            P("layer", "latent", None),
            P("layer", "latent", None),
            P("layer", None, "latent"),
            P("layer", "latent", None),
            P("latent"),
            P(None, "latent"),
        ),
        out_specs=(P("layer", None, "latent"), P("layer", "latent", None), P("latent")),
        check_vma=False,
    )
```

```python
import functools

import jax
import jax.numpy as jnp
from jax import lax
from jax.experimental import pallas as pl
from jax.experimental.pallas import tpu as pltpu
from jax.sharding import PartitionSpec as P

KEEP = 64


def take(values, lanes):
    return jnp.take_along_axis(values, lanes, axis=1, mode="promise_in_bounds")


def tiles_of(array):
    return [array[:, at : at + 128] for at in range(0, array.shape[1], 128)]


def rank_kernel(order_ref, mask_ref, rank_ref, slot_ref):
    latents = mask_ref.shape[1]
    blocks = order_ref.shape[0]
    rows = mask_ref.shape[0] // blocks
    half = rows // 2
    f32, bf16, i32 = jnp.float32, jnp.bfloat16, jnp.int32
    shape = (latents, latents)
    row, column = lax.broadcasted_iota(i32, shape, 0), lax.broadcasted_iota(i32, shape, 1)
    upper = (row <= column).astype(f32).astype(bf16)
    row, column = row[:, :128], column[:, :128]
    ahead = (row < 16 * column).astype(f32).astype(bf16)
    bits = jnp.where(row // 16 == column, jnp.left_shift(1, row % 16), 0).astype(f32).astype(bf16)
    group = 4
    for first in range(0, blocks, group):
        mask = [mask_ref[pl.ds(pl.multiple_of(order_ref[first + k] * rows, rows), rows), :] for k in range(group)]
        mask = jnp.concatenate(mask, axis=0)
        ones = mask.astype(f32).astype(bf16)
        count = jnp.dot(ones, upper, preferred_element_type=f32).astype(i32)
        rank_ref[first * rows : (first + group) * rows, :] = jnp.where(mask > 0, count - 1, -1)
        before = jnp.dot(ones, ahead, preferred_element_type=f32).astype(i32)
        word = jnp.dot(ones, bits, preferred_element_type=f32).astype(i32)
        lane = lax.broadcasted_iota(i32, (group * rows, 128), 1)
        place = lane % KEEP
        segment = jnp.zeros(lane.shape, i32)
        base = jnp.zeros(lane.shape, i32)
        for step in (16, 8, 4, 2, 1):
            seen = take(before, segment + step)
            segment += jnp.where(seen <= place, step, 0)
            base = jnp.where(seen <= place, seen, base)
        word = take(word, segment)
        left = place - base
        at = segment * 16
        for step in (8, 4, 2, 1):
            low = word & ((1 << step) - 1)
            ones = low
            if step > 1:
                ones = (ones & 0x5555) + ((ones >> 1) & 0x5555)
            if step > 2:
                ones = (ones & 0x3333) + ((ones >> 2) & 0x3333)
            if step > 4:
                ones = (ones & 0x0F0F) + ((ones >> 4) & 0x0F0F)
            past = left >= ones
            left = jnp.where(past, left - ones, left)
            word = jnp.where(past, word >> step, low)
            at += jnp.where(past, step, 0)
        for k in range(group):
            one, two = at[k * rows : k * rows + half], at[k * rows + half : (k + 1) * rows]
            to = (first + k) * half
            slot_ref[to : to + half, :] = jnp.where(lane[:half] < KEEP, one, two)


def squeeze(full, slot):
    half = slot.shape[0]
    lane = lax.broadcasted_iota(jnp.int32, (half, 128), 1)
    tile, at = slot // 128, slot % 128
    out = jnp.zeros((half, 128), jnp.float32)
    for number, part in enumerate(tiles_of(full)):
        got = jnp.where(lane < KEEP, take(part[:half], at), take(part[half:], at))
        out = jnp.where(tile == number, got, out)
    return out


def spread(packed, rank):
    half = packed.shape[0]
    parts = []
    for number, place in enumerate(tiles_of(rank)):
        at = jnp.maximum(place, 0)
        got = jnp.concatenate([take(packed, at[:half]), take(packed, at[half:] + KEEP)], axis=0)
        parts.append(jnp.where(place >= 0, got, 0.0))
    return jnp.concatenate(parts, axis=1)


def read(pieces, places, columns=slice(None)):
    parts = [pieces[n][:, columns] if lead is None else pieces[n][lead, :, columns] for n, lead in places]
    return jnp.concatenate(parts, axis=0)


def term_kernel(acts_at, cots_at, first, earlier, *refs):
    out_ref = refs[-1]
    given = refs[len(refs) - 1 - earlier : -1]
    pieces = refs[: len(refs) - 4 - earlier]
    enc_ref, dec_ref, slot_ref = refs[len(pieces) : len(pieces) + 3]
    chunk = 0
    for ref in given:
        out_ref[chunk : chunk + ref.shape[0]] = ref[...]
        chunk += ref.shape[0]
    pre = jnp.dot(read(pieces, acts_at), enc_ref[...], preferred_element_type=jnp.float32)
    cot = lax.dot_general(
        read(pieces, cots_at), dec_ref[...], (((1,), (1,)), ((), ())), preferred_element_type=jnp.float32
    )
    rows, half = 64, 32
    tokens = pre.shape[0]
    for block in range(tokens // rows):
        slot = slot_ref[first // 2 + block * half : first // 2 + (block + 1) * half, :]
        at = slice(block * rows, (block + 1) * rows)
        to = slice(block % 2 * half, (block % 2 + 1) * half)
        out_ref[chunk + block // 2, to, :] = squeeze(pre[at], slot).astype(out_ref.dtype)
        out_ref[chunk + tokens // 128 + block // 2, to, :] = squeeze(cot[at], slot).astype(out_ref.dtype)


def sum_kernel(place_ref, terms_ref, slot_ref, bias_ref, out_ref):
    total = jnp.sum(terms_ref[...].astype(jnp.float32), axis=0)
    half = total.shape[0]
    bias = jnp.broadcast_to(bias_ref[...], (2 * half, bias_ref.shape[1]))
    slot = slot_ref[pl.ds(pl.multiple_of(place_ref[0] * half, half), half), :]
    total += jnp.where(place_ref[1] > 0, squeeze(bias, slot), 0.0)
    out_ref[...] = jnp.broadcast_to(total.astype(out_ref.dtype)[None], out_ref.shape)


def grad_kernel(acts_at, cots_at, sizes, *refs):
    sums_ref, rank_ref = refs[:2]
    pieces = refs[2:-8]
    enc_ref, dec_ref, bias_ref, code_ref, pre_ref, enc_tile, dec_tile, sems = refs[-8:]
    total = jnp.zeros(bias_ref.shape, jnp.float32)
    chunk = token = 0
    for size in sizes:
        for block in range(size // 64):
            rank = rank_ref[token : token + 64, :]
            at = slice(block % 2 * 32, (block % 2 + 1) * 32)
            code = sums_ref[chunk + block // 2, at, :].astype(jnp.float32)
            code_ref[token : token + 64, :] = spread(code, rank).astype(code_ref.dtype)
            pre = sums_ref[chunk + size // 128 + block // 2, at, :].astype(jnp.float32)
            pre = spread(pre, rank)
            pre_ref[token : token + 64, :] = pre.astype(pre_ref.dtype)
            total += jnp.sum(pre, axis=0, keepdims=True)
            token += 64
        chunk += size // 64
    bias_ref[...] = total

    cut = enc_tile.shape[1]
    over_tokens = (((0,), (0,)), ((), ()))
    out = [[], []]
    for step in range(enc_ref.shape[0] // cut):
        columns = slice(step * cut, (step + 1) * cut)
        side = step % 2
        for copy in out[side]:
            copy.wait()
        dec = lax.dot_general(
            code_ref[...], read(pieces, cots_at, columns), over_tokens, preferred_element_type=jnp.float32
        )
        dec_tile[side] = dec.astype(dec_tile.dtype)
        enc = lax.dot_general(
            read(pieces, acts_at, columns), pre_ref[...], over_tokens, preferred_element_type=jnp.float32
        )
        enc_tile[side] = enc.astype(enc_tile.dtype)
        out[side] = [
            pltpu.make_async_copy(dec_tile.at[side], dec_ref.at[:, columns], sems.at[0, side]),
            pltpu.make_async_copy(enc_tile.at[side], enc_ref.at[columns, :], sems.at[1, side]),
        ]
        for copy in out[side]:
            copy.start()
    for copy in out[0] + out[1]:
        copy.wait()


def params(mib):
    return pltpu.CompilerParams(vmem_limit_bytes=mib * 1024 * 1024)


def whole():
    return pl.BlockSpec(memory_space=pltpu.VMEM)


def device(x, y, core):
    return (x * 4 + y) * 2 + core


def hop(dx, dy, dcore):
    return [
        (device(x, y, core), device((x + dx) % 2, (y + dy) % 4, (core + dcore) % 2))
        for x in range(2)
        for y in range(4)
        for core in range(2)
    ]


def east(values):
    return lax.ppermute(values, "latent", hop(1, 0, 0))


def up(values):
    return lax.ppermute(values, "latent", hop(0, 1, 0))


def down(values):
    return lax.ppermute(values, "latent", hop(0, -1, 0))


def twin(values):
    return lax.ppermute(values, "latent", hop(0, 0, 1))


ORIGINS = [
    (dx, dy, core)
    for dx, dy in ((0, 0), (1, 0), (0, 3), (0, 1), (0, 2), (1, 3), (1, 1), (1, 2))
    for core in (0, 1)
]


def stack_kernel(first_ref, second_ref, out_ref):
    out_ref[0] = first_ref[...]
    out_ref[1] = second_ref[...]


def local(activations, cotangents, enc_weight, dec_weight, enc_bias, active_mask):
    tokens, latents = active_mask.shape
    rows, width = activations.shape[1:]
    blocks = tokens // rows
    half = rows // 2
    f32, bf16 = jnp.float32, jnp.bfloat16
    acts, cots = activations[0], cotangents[0]
    enc, dec = enc_weight[0], dec_weight[0]

    here = lax.axis_index("latent").astype(jnp.int32)
    x, y, core = here // 8, here // 2 % 4, here % 2
    far_x, far_y, far_core = (jnp.array(column, jnp.int32) for column in zip(*ORIGINS))
    order = device((x + far_x) % 2, (y + far_y) % 4, (core + far_core) % 2)
    layer = lax.axis_index("layer").astype(jnp.int32)
    is_code = (layer < 4) | ((layer >= 8) & (layer < 11)) | (layer == 14)
    block = jnp.where(layer < 4, layer, jnp.where(layer < 11, layer - 4, 7))
    block = jnp.where(is_code, block, 0)
    place = jnp.stack([block, is_code.astype(jnp.int32)])
    smem = pl.BlockSpec(memory_space=pltpu.SMEM)

    own = pl.pallas_call(
        stack_kernel,
        in_specs=[whole(), whole()],
        out_specs=whole(),
        out_shape=jax.ShapeDtypeStruct((2, rows, width), bf16),
        compiler_params=params(4),
        name="stack",
    )(acts, cots)
    rank, slot = pl.pallas_call(
        rank_kernel,
        in_specs=[smem, whole()],
        out_specs=[whole(), whole()],
        out_shape=[
            jax.ShapeDtypeStruct((tokens, latents), jnp.int32),
            jax.ShapeDtypeStruct((tokens // 2, 128), jnp.int32),
        ],
        compiler_params=params(12),
        cost_estimate=pl.CostEstimate(flops=3 * 10**9, bytes_accessed=4 * 10**6, transcendentals=0),
        name="ranks",
    )(order, active_mask)

    a_x = east(acts)
    low, high = up(own), down(own)
    c_x = east(cots)
    a_x_low, a_x_high = up(a_x), down(a_x)
    low, high, rank, slot, place = lax.optimization_barrier((low, high, rank, slot, place))
    far_1, far_2 = up(low[:, :half]), down(high[:, half:])
    c_x_low, c_x_high = east(low[1]), east(high[1])
    a_x_far_1, a_x_far_2 = up(a_x_low[:half]), down(a_x_high[half:])
    far_1, far_2, own = lax.optimization_barrier((far_1, far_2, own))
    c_x_far = east(jnp.concatenate([far_1[1], far_2[1]]))

    pieces = [own, a_x, c_x, low, high]
    pieces += [far_1, far_2, a_x_low, a_x_high, c_x_low, c_x_high]
    pieces += [a_x_far_1, a_x_far_2, c_x_far]
    doubled = [piece for one in pieces for piece in (one, twin(one))]
    sizes = (512, 384, 128)
    acts_at = [
        [[(0, 0)], [(1, None)], [(3, 0)], [(4, 0)]],
        [[(5, 0), (6, 0)], [(7, None)], [(8, None)]],
        [[(11, None), (12, None)]],
    ]
    cots_at = [
        [[(0, 1)], [(2, None)], [(3, 1)], [(4, 1)]],
        [[(5, 1), (6, 1)], [(9, None)], [(10, None)]],
        [[(13, None)]],
    ]

    def with_twins(items, first=0):
        return [(2 * (n - first) + core, lead) for item in items for core in (0, 1) for n, lead in item]

    terms = []
    spans = ((0, 5), (5, 11), (11, 14))
    for number, (first, last) in enumerate(spans):
        size, start = sizes[number], sum(sizes[:number])
        used = doubled[2 * first : 2 * last]
        at = with_twins(acts_at[number], first), with_twins(cots_at[number], first)
        earlier = terms if number == 2 else []
        given = sum(array.shape[0] for array in earlier)
        kernel = functools.partial(term_kernel, *at, start, len(earlier))
        out = pl.pallas_call(
            kernel,
            in_specs=[whole()] * (len(used) + 3 + len(earlier)),
            out_specs=whole(),
            out_shape=jax.ShapeDtypeStruct((given + size // 64, 64, 128), bf16),
            compiler_params=params(12),
            cost_estimate=pl.CostEstimate(
                flops=4 * size * width * latents, bytes_accessed=4 * size * width, transcendentals=0
            ),
            name=("near", "middle", "far")[number],
        )(*used, enc, dec, slot, *earlier)
        terms = terms + [out]

    mine = lax.all_to_all(terms[2], "layer", 0, 0)
    sums = pl.pallas_call(
        sum_kernel,
        in_specs=[smem, whole(), whole(), whole()],
        out_specs=whole(),
        out_shape=jax.ShapeDtypeStruct((blocks, rows, 128), bf16),
        compiler_params=params(4),
        name="sums",
    )(place, mine, slot, enc_bias[None, :])
    sums = lax.all_to_all(sums, "layer", 0, 0)

    cut = 256
    all_acts = [at for items in acts_at for at in with_twins(items)]
    all_cots = [at for items in cots_at for at in with_twins(items)]
    hbm = pl.BlockSpec(memory_space=pl.ANY)
    enc_grad, dec_grad, bias_grad = pl.pallas_call(
        functools.partial(grad_kernel, all_acts, all_cots, sizes),
        in_specs=[whole()] * (2 + len(doubled)),
        out_specs=[hbm, hbm, whole()],
        out_shape=[
            jax.ShapeDtypeStruct((width, latents), bf16),
            jax.ShapeDtypeStruct((latents, width), bf16),
            jax.ShapeDtypeStruct((1, latents), f32),
        ],
        scratch_shapes=[
            pltpu.VMEM((tokens, latents), bf16),
            pltpu.VMEM((tokens, latents), bf16),
            pltpu.VMEM((2, cut, latents), bf16),
            pltpu.VMEM((2, latents, cut), bf16),
            pltpu.SemaphoreType.DMA((2, 2)),
        ],
        compiler_params=params(16),
        name="grads",
    )(sums, rank, *doubled)
    return enc_grad[None], dec_grad[None], bias_grad[0]


def solution(mesh):
    return jax.shard_map(
        local,
        mesh=mesh,
        in_specs=(
            P("layer", "latent", None),
            P("layer", "latent", None),
            P("layer", None, "latent"),
            P("layer", "latent", None),
            P("latent"),
            P(None, "latent"),
        ),
        out_specs=(P("layer", None, "latent"), P("layer", "latent", None), P("latent")),
        check_vma=False,
    )
```

```python
import functools

import jax
import jax.numpy as jnp
from jax import lax
from jax.experimental import pallas as pl
from jax.experimental.pallas import tpu as pltpu
from jax.sharding import PartitionSpec as P

KEEP = 64


def take(values, lanes):
    return jnp.take_along_axis(values, lanes, axis=1, mode="promise_in_bounds")


def tiles_of(array):
    return [array[:, at : at + 128] for at in range(0, array.shape[1], 128)]


def rank_kernel(order_ref, mask_ref, rank_ref, slot_ref):
    latents = mask_ref.shape[1]
    blocks = order_ref.shape[0]
    rows = mask_ref.shape[0] // blocks
    half = rows // 2
    f32, bf16, i32 = jnp.float32, jnp.bfloat16, jnp.int32
    shape = (latents, latents)
    row, column = lax.broadcasted_iota(i32, shape, 0), lax.broadcasted_iota(i32, shape, 1)
    upper = (row <= column).astype(f32).astype(bf16)
    row, column = row[:, :128], column[:, :128]
    ahead = (row < 16 * column).astype(f32).astype(bf16)
    bits = jnp.where(row // 16 == column, jnp.left_shift(1, row % 16), 0).astype(f32).astype(bf16)
    group = 4
    for first in range(0, blocks, group):
        mask = [mask_ref[pl.ds(pl.multiple_of(order_ref[first + k] * rows, rows), rows), :] for k in range(group)]
        mask = jnp.concatenate(mask, axis=0)
        ones = mask.astype(f32).astype(bf16)
        count = jnp.dot(ones, upper, preferred_element_type=f32).astype(i32)
        rank_ref[first * rows : (first + group) * rows, :] = jnp.where(mask > 0, count - 1, -1)
        before = jnp.dot(ones, ahead, preferred_element_type=f32).astype(i32)
        word = jnp.dot(ones, bits, preferred_element_type=f32).astype(i32)
        lane = lax.broadcasted_iota(i32, (group * rows, 128), 1)
        place = lane % KEEP
        segment = jnp.zeros(lane.shape, i32)
        base = jnp.zeros(lane.shape, i32)
        for step in (16, 8, 4, 2, 1):
            seen = take(before, segment + step)
            segment += jnp.where(seen <= place, step, 0)
            base = jnp.where(seen <= place, seen, base)
        word = take(word, segment)
        left = place - base
        at = segment * 16
        for step in (8, 4, 2, 1):
            low = word & ((1 << step) - 1)
            ones = low
            if step > 1:
                ones = (ones & 0x5555) + ((ones >> 1) & 0x5555)
            if step > 2:
                ones = (ones & 0x3333) + ((ones >> 2) & 0x3333)
            if step > 4:
                ones = (ones & 0x0F0F) + ((ones >> 4) & 0x0F0F)
            past = left >= ones
            left = jnp.where(past, left - ones, left)
            word = jnp.where(past, word >> step, low)
            at += jnp.where(past, step, 0)
        for k in range(group):
            one, two = at[k * rows : k * rows + half], at[k * rows + half : (k + 1) * rows]
            to = (first + k) * half
            slot_ref[to : to + half, :] = jnp.where(lane[:half] < KEEP, one, two)


def squeeze(full, slot):
    half = slot.shape[0]
    lane = lax.broadcasted_iota(jnp.int32, (half, 128), 1)
    tile, at = slot // 128, slot % 128
    out = jnp.zeros((half, 128), jnp.float32)
    for number, part in enumerate(tiles_of(full)):
        got = jnp.where(lane < KEEP, take(part[:half], at), take(part[half:], at))
        out = jnp.where(tile == number, got, out)
    return out


def spread(packed, rank):
    half = packed.shape[0]
    parts = []
    for number, place in enumerate(tiles_of(rank)):
        at = jnp.maximum(place, 0)
        got = jnp.concatenate([take(packed, at[:half]), take(packed, at[half:] + KEEP)], axis=0)
        parts.append(jnp.where(place >= 0, got, 0.0))
    return jnp.concatenate(parts, axis=1)


def read(pieces, places, columns=slice(None)):
    return jnp.concatenate([pieces[n][first:last, columns] for n, first, last in places], axis=0)


def term_kernel(acts_at, cots_at, first, earlier, *refs):
    out_ref = refs[-1]
    given = refs[len(refs) - 1 - earlier : -1]
    pieces = refs[: len(refs) - 4 - earlier]
    enc_ref, dec_ref, slot_ref = refs[len(pieces) : len(pieces) + 3]
    chunk = 0
    for ref in given:
        out_ref[chunk : chunk + ref.shape[0]] = ref[...]
        chunk += ref.shape[0]
    pre = jnp.dot(read(pieces, acts_at), enc_ref[...], preferred_element_type=jnp.float32)
    cot = lax.dot_general(
        read(pieces, cots_at), dec_ref[...], (((1,), (1,)), ((), ())), preferred_element_type=jnp.float32
    )
    rows, half = 64, 32
    tokens = pre.shape[0]
    for block in range(tokens // rows):
        slot = slot_ref[first // 2 + block * half : first // 2 + (block + 1) * half, :]
        at = slice(block * rows, (block + 1) * rows)
        to = slice(block % 2 * half, (block % 2 + 1) * half)
        out_ref[chunk + block // 2, to, :] = squeeze(pre[at], slot).astype(out_ref.dtype)
        out_ref[chunk + tokens // 128 + block // 2, to, :] = squeeze(cot[at], slot).astype(out_ref.dtype)


def sum_kernel(place_ref, terms_ref, slot_ref, bias_ref, out_ref):
    total = jnp.sum(terms_ref[...].astype(jnp.float32), axis=0)
    half = total.shape[0]
    bias = jnp.broadcast_to(bias_ref[...], (2 * half, bias_ref.shape[1]))
    slot = slot_ref[pl.ds(pl.multiple_of(place_ref[0] * half, half), half), :]
    total += jnp.where(place_ref[1] > 0, squeeze(bias, slot), 0.0)
    out_ref[...] = jnp.broadcast_to(total.astype(out_ref.dtype)[None], out_ref.shape)


def grad_kernel(acts_at, cots_at, sizes, *refs):
    sums_ref, rank_ref = refs[:2]
    pieces = refs[2:-8]
    enc_ref, dec_ref, bias_ref, code_ref, pre_ref, enc_tile, dec_tile, sems = refs[-8:]
    total = jnp.zeros(bias_ref.shape, jnp.float32)
    chunk = token = 0
    for size in sizes:
        for block in range(size // 64):
            rank = rank_ref[token : token + 64, :]
            at = slice(block % 2 * 32, (block % 2 + 1) * 32)
            code = sums_ref[chunk + block // 2, at, :].astype(jnp.float32)
            code_ref[token : token + 64, :] = spread(code, rank).astype(code_ref.dtype)
            pre = sums_ref[chunk + size // 128 + block // 2, at, :].astype(jnp.float32)
            pre = spread(pre, rank)
            pre_ref[token : token + 64, :] = pre.astype(pre_ref.dtype)
            total += jnp.sum(pre, axis=0, keepdims=True)
            token += 64
        chunk += size // 64
    bias_ref[...] = total

    cut = enc_tile.shape[1]
    over_tokens = (((0,), (0,)), ((), ()))
    out = [[], []]
    for step in range(enc_ref.shape[0] // cut):
        columns = slice(step * cut, (step + 1) * cut)
        side = step % 2
        for copy in out[side]:
            copy.wait()
        dec = lax.dot_general(
            code_ref[...], read(pieces, cots_at, columns), over_tokens, preferred_element_type=jnp.float32
        )
        dec_tile[side] = dec.astype(dec_tile.dtype)
        enc = lax.dot_general(
            read(pieces, acts_at, columns), pre_ref[...], over_tokens, preferred_element_type=jnp.float32
        )
        enc_tile[side] = enc.astype(enc_tile.dtype)
        out[side] = [
            pltpu.make_async_copy(dec_tile.at[side], dec_ref.at[:, columns], sems.at[0, side]),
            pltpu.make_async_copy(enc_tile.at[side], enc_ref.at[columns, :], sems.at[1, side]),
        ]
        for copy in out[side]:
            copy.start()
    for copy in out[0] + out[1]:
        copy.wait()


def params(mib):
    return pltpu.CompilerParams(vmem_limit_bytes=mib * 1024 * 1024)


def whole():
    return pl.BlockSpec(memory_space=pltpu.VMEM)


def device(x, y, core):
    return (x * 4 + y) * 2 + core


def hop(dx, dy, dcore):
    return [
        (device(x, y, core), device((x + dx) % 2, (y + dy) % 4, (core + dcore) % 2))
        for x in range(2)
        for y in range(4)
        for core in range(2)
    ]


def east(values):
    return lax.ppermute(values, "latent", hop(1, 0, 0))


def up(values):
    return lax.ppermute(values, "latent", hop(0, 1, 0))


def down(values):
    return lax.ppermute(values, "latent", hop(0, -1, 0))


def twin(values):
    return lax.ppermute(values, "latent", hop(0, 0, 1))


ORIGINS = [
    (dx, dy, core)
    for dx, dy in ((0, 0), (1, 0), (0, 3), (0, 1), (1, 3), (1, 1), (0, 2), (1, 2))
    for core in (0, 1)
]


def pack_kernel(outs, *refs):
    sems = refs[-1]
    out_refs = refs[len(refs) - 1 - len(outs) : -1]
    copies = []
    for out_ref, parts in zip(out_refs, outs):
        at = 0
        for n, first, last in parts:
            here = out_ref.at[at : at + last - first]
            copies.append(pltpu.make_async_copy(refs[n].at[first:last], here, sems.at[len(copies)]))
            at += last - first
    for copy in copies:
        copy.start()
    for copy in copies:
        copy.wait()


def pack_all(*groups):
    given, outs = [], []
    for group in groups:
        outs.append([])
        for part in group:
            array, first, last = part if isinstance(part, tuple) else (part, 0, part.shape[0])
            outs[-1].append((len(given), first, last))
            given.append(array)
    width, dtype = given[0].shape[1], given[0].dtype
    totals = [sum(last - first for _, first, last in parts) for parts in outs]
    hbm = pl.BlockSpec(memory_space=pl.ANY)
    return pl.pallas_call(
        functools.partial(pack_kernel, outs),
        in_specs=[hbm] * len(given),
        out_specs=[hbm] * len(outs),
        out_shape=[jax.ShapeDtypeStruct((total, width), dtype) for total in totals],
        scratch_shapes=[pltpu.SemaphoreType.DMA((len(given),))],
        compiler_params=params(2),
        cost_estimate=pl.CostEstimate(flops=0, bytes_accessed=sum(totals) * 8192, transcendentals=0),
        name="pack",
    )(*given)


def pack(*parts):
    return pack_all(parts)[0]


def local(activations, cotangents, enc_weight, dec_weight, enc_bias, active_mask):
    tokens, latents = active_mask.shape
    rows, width = activations.shape[1:]
    blocks = tokens // rows
    half = rows // 2
    f32, bf16 = jnp.float32, jnp.bfloat16
    acts, cots = activations[0], cotangents[0]
    enc, dec = enc_weight[0], dec_weight[0]

    here = lax.axis_index("latent").astype(jnp.int32)
    x, y, core = here // 8, here // 2 % 4, here % 2
    far_x, far_y, far_core = (jnp.array(column, jnp.int32) for column in zip(*ORIGINS))
    order = device((x + far_x) % 2, (y + far_y) % 4, (core + far_core) % 2)
    layer = lax.axis_index("layer").astype(jnp.int32)
    is_code = (layer < 4) | ((layer >= 8) & (layer % 4 < 2))
    block = jnp.where(layer < 8, layer, layer // 2 + layer % 2)
    block = jnp.where(is_code, block, 0)
    place = jnp.stack([block, is_code.astype(jnp.int32)])
    smem = pl.BlockSpec(memory_space=pltpu.SMEM)

    hbm = pl.BlockSpec(memory_space=pl.ANY)
    tie = lax.optimization_barrier
    rank, slot = pl.pallas_call(
        rank_kernel,
        in_specs=[smem, whole()],
        out_specs=[whole(), whole()],
        out_shape=[
            jax.ShapeDtypeStruct((tokens, latents), jnp.int32),
            jax.ShapeDtypeStruct((tokens // 2, 128), jnp.int32),
        ],
        compiler_params=params(12),
        cost_estimate=pl.CostEstimate(flops=3 * 10**9, bytes_accessed=4 * 10**6, transcendentals=0),
        name="ranks",
    )(order, active_mask)
    a_x = east(acts)
    c_low, c_high = up(cots), down(cots)
    a_low, a_high = up(acts), down(acts)
    a_x, cots_later = tie((a_x, cots))
    c_x = east(cots_later)
    c_x_near = east(pack(c_low, c_high))
    sent = pack_all([a_x, (c_low, 0, half)], [a_x, (c_high, half, rows)])
    *sent, a_low, a_high, rank, slot, place = tie((*sent, a_low, a_high, rank, slot, place))
    third_low, third_high = up(sent[0]), down(sent[1])
    sent = pack_all(
        [(third_low, rows, rows + half), (third_high, rows, rows + half)],
        [(a_low, 0, half), (third_low, 0, half)],
        [(a_high, half, rows), (third_high, half, rows)],
    )
    c_x_far, fourth_low, fourth_high = east(sent[0]), up(sent[1]), down(sent[2])

    *first, _ = tie((acts, cots, a_x, c_low, c_high, a_low, a_high, c_x, c_x))
    first = pack(*first)
    second = pack(third_low, third_high, c_x_near)
    sizes = (512, 256, 256)
    acts_at = [
        [[(0, k * rows, (k + 1) * rows)] for k in (0, 2, 5, 6)],
        [[(1, 0, 64)], [(1, 96, 160)]],
        [[(2, 0, 32), (2, 64, 96)], [(2, 32, 64), (2, 96, 128)]],
    ]
    cots_at = [
        [[(0, k * rows, (k + 1) * rows)] for k in (1, 7, 3, 4)],
        [[(1, 192, 256)], [(1, 256, 320)]],
        [[(1, 64, 96), (1, 160, 192)], [(2, 128, 192)]],
    ]

    def with_twins(items, first=0):
        return [(2 * (n - first) + core, *at) for item in items for core in (0, 1) for n, *at in item]

    def terms_of(number, earlier, used):
        size, start, first_piece = sizes[number], sum(sizes[:number]), min(number, 1)
        at = with_twins(acts_at[number], first_piece), with_twins(cots_at[number], first_piece)
        given = sum(array.shape[0] for array in earlier)
        return pl.pallas_call(
            functools.partial(term_kernel, *at, start, len(earlier)),
            in_specs=[whole()] * (len(used) + 3 + len(earlier)),
            out_specs=whole(),
            out_shape=jax.ShapeDtypeStruct((given + size // 64, 64, 128), bf16),
            compiler_params=params(12),
            cost_estimate=pl.CostEstimate(
                flops=4 * size * width * latents, bytes_accessed=4 * size * width, transcendentals=0
            ),
            name=("near", "middle", "far")[number],
        )(*used, enc, dec, slot, *earlier)

    doubled = [first, twin(first)]
    terms = terms_of(0, [], doubled)
    doubled += [second, twin(second)]
    terms = terms_of(1, [terms], doubled[2:])
    *doubled, terms, fourth_low, fourth_high, c_x_far = tie((*doubled, terms, fourth_low, fourth_high, c_x_far))
    last = pack(fourth_low, fourth_high, c_x_far)
    doubled += [last, twin(last)]
    terms = terms_of(2, [terms], doubled[2:])

    mine = lax.all_to_all(terms, "layer", 0, 0)
    sums = pl.pallas_call(
        sum_kernel,
        in_specs=[smem, whole(), whole(), whole()],
        out_specs=whole(),
        out_shape=jax.ShapeDtypeStruct((blocks, rows, 128), bf16),
        compiler_params=params(4),
        name="sums",
    )(place, mine, slot, enc_bias[None, :])
    sums = lax.all_to_all(sums, "layer", 0, 0)

    cut = 256
    all_acts = [at for items in acts_at for at in with_twins(items)]
    all_cots = [at for items in cots_at for at in with_twins(items)]
    enc_grad, dec_grad, bias_grad = pl.pallas_call(
        functools.partial(grad_kernel, all_acts, all_cots, sizes),
        in_specs=[whole()] * (2 + len(doubled)),
        out_specs=[pl.BlockSpec(memory_space=pl.ANY)] * 2 + [whole()],
        out_shape=[
            jax.ShapeDtypeStruct((width, latents), bf16),
            jax.ShapeDtypeStruct((latents, width), bf16),
            jax.ShapeDtypeStruct((1, latents), f32),
        ],
        scratch_shapes=[
            pltpu.VMEM((tokens, latents), bf16),
            pltpu.VMEM((tokens, latents), bf16),
            pltpu.VMEM((2, cut, latents), bf16),
            pltpu.VMEM((2, latents, cut), bf16),
            pltpu.SemaphoreType.DMA((2, 2)),
        ],
        compiler_params=params(16),
        name="grads",
    )(sums, rank, *doubled)
    return enc_grad[None], dec_grad[None], bias_grad[0]


def solution(mesh):
    return jax.shard_map(
        local,
        mesh=mesh,
        in_specs=(
            P("layer", "latent", None),
            P("layer", "latent", None),
            P("layer", None, "latent"),
            P("layer", "latent", None),
            P("latent"),
            P(None, "latent"),
        ),
        out_specs=(P("layer", None, "latent"), P("layer", "latent", None), P("latent")),
        check_vma=False,
    )
```

```python
import functools

import jax
import jax.numpy as jnp
from jax import lax
from jax.experimental import pallas as pl
from jax.experimental.pallas import tpu as pltpu
from jax.sharding import PartitionSpec as P

KEEP = 64


def take(values, lanes):
    return jnp.take_along_axis(values, lanes, axis=1, mode="promise_in_bounds")


def tiles_of(array):
    return [array[:, at : at + 128] for at in range(0, array.shape[1], 128)]


def rank_kernel(order_ref, mask_ref, rank_ref, slot_ref):
    latents = mask_ref.shape[1]
    blocks = order_ref.shape[0]
    rows = mask_ref.shape[0] // blocks
    half = rows // 2
    f32, bf16, i32 = jnp.float32, jnp.bfloat16, jnp.int32
    shape = (latents, latents)
    row, column = lax.broadcasted_iota(i32, shape, 0), lax.broadcasted_iota(i32, shape, 1)
    upper = (row <= column).astype(f32).astype(bf16)
    row, column = row[:, :128], column[:, :128]
    ahead = (row < 16 * column).astype(f32).astype(bf16)
    bits = jnp.where(row // 16 == column, jnp.left_shift(1, row % 16), 0).astype(f32).astype(bf16)
    group = 4
    for first in range(0, blocks, group):
        mask = [mask_ref[pl.ds(pl.multiple_of(order_ref[first + k] * rows, rows), rows), :] for k in range(group)]
        mask = jnp.concatenate(mask, axis=0)
        ones = mask.astype(f32).astype(bf16)
        count = jnp.dot(ones, upper, preferred_element_type=f32).astype(i32)
        rank_ref[first * rows : (first + group) * rows, :] = jnp.where(mask > 0, count - 1, -1)
        before = jnp.dot(ones, ahead, preferred_element_type=f32).astype(i32)
        word = jnp.dot(ones, bits, preferred_element_type=f32).astype(i32)
        lane = lax.broadcasted_iota(i32, (group * rows, 128), 1)
        place = lane % KEEP
        segment = jnp.zeros(lane.shape, i32)
        base = jnp.zeros(lane.shape, i32)
        for step in (16, 8, 4, 2, 1):
            seen = take(before, segment + step)
            segment += jnp.where(seen <= place, step, 0)
            base = jnp.where(seen <= place, seen, base)
        word = take(word, segment)
        left = place - base
        at = segment * 16
        for step in (8, 4, 2, 1):
            low = word & ((1 << step) - 1)
            ones = low
            if step > 1:
                ones = (ones & 0x5555) + ((ones >> 1) & 0x5555)
            if step > 2:
                ones = (ones & 0x3333) + ((ones >> 2) & 0x3333)
            if step > 4:
                ones = (ones & 0x0F0F) + ((ones >> 4) & 0x0F0F)
            past = left >= ones
            left = jnp.where(past, left - ones, left)
            word = jnp.where(past, word >> step, low)
            at += jnp.where(past, step, 0)
        for k in range(group):
            one, two = at[k * rows : k * rows + half], at[k * rows + half : (k + 1) * rows]
            to = (first + k) * half
            slot_ref[to : to + half, :] = jnp.where(lane[:half] < KEEP, one, two)


def squeeze(full, slot):
    half = slot.shape[0]
    lane = lax.broadcasted_iota(jnp.int32, (half, 128), 1)
    tile, at = slot // 128, slot % 128
    out = jnp.zeros((half, 128), jnp.float32)
    for number, part in enumerate(tiles_of(full)):
        got = jnp.where(lane < KEEP, take(part[:half], at), take(part[half:], at))
        out = jnp.where(tile == number, got, out)
    return out


def spread(packed, rank):
    half = packed.shape[0]
    parts = []
    for number, place in enumerate(tiles_of(rank)):
        at = jnp.maximum(place, 0)
        got = jnp.concatenate([take(packed, at[:half]), take(packed, at[half:] + KEEP)], axis=0)
        parts.append(jnp.where(place >= 0, got, 0.0))
    return jnp.concatenate(parts, axis=1)


def read(pieces, places, columns=slice(None)):
    return jnp.concatenate([pieces[n][first:last, columns] for n, first, last in places], axis=0)


def term_kernel(acts_at, cots_at, first, earlier, *refs):
    out_ref = refs[-1]
    given = refs[len(refs) - 1 - earlier : -1]
    pieces = refs[: len(refs) - 4 - earlier]
    enc_ref, dec_ref, slot_ref = refs[len(pieces) : len(pieces) + 3]
    chunk = 0
    for ref in given:
        out_ref[chunk : chunk + ref.shape[0]] = ref[...]
        chunk += ref.shape[0]
    pre = jnp.dot(read(pieces, acts_at), enc_ref[...], preferred_element_type=jnp.float32)
    cot = lax.dot_general(
        read(pieces, cots_at), dec_ref[...], (((1,), (1,)), ((), ())), preferred_element_type=jnp.float32
    )
    rows, half = 64, 32
    tokens = pre.shape[0]
    for block in range(tokens // rows):
        slot = slot_ref[first // 2 + block * half : first // 2 + (block + 1) * half, :]
        at = slice(block * rows, (block + 1) * rows)
        to = slice(block % 2 * half, (block % 2 + 1) * half)
        out_ref[chunk + block // 2, to, :] = squeeze(pre[at], slot).astype(out_ref.dtype)
        out_ref[chunk + tokens // 128 + block // 2, to, :] = squeeze(cot[at], slot).astype(out_ref.dtype)


def sum_kernel(place_ref, terms_ref, slot_ref, bias_ref, out_ref):
    total = jnp.sum(terms_ref[...].astype(jnp.float32), axis=0)
    half = total.shape[0]
    bias = jnp.broadcast_to(bias_ref[...], (2 * half, bias_ref.shape[1]))
    slot = slot_ref[pl.ds(pl.multiple_of(place_ref[0] * half, half), half), :]
    total += jnp.where(place_ref[1] > 0, squeeze(bias, slot), 0.0)
    out_ref[...] = jnp.broadcast_to(total.astype(out_ref.dtype)[None], out_ref.shape)


def grad_kernel(acts_at, cots_at, sizes, *refs):
    sums_ref, rank_ref = refs[:2]
    pieces = refs[2:-8]
    enc_ref, dec_ref, bias_ref, code_ref, pre_ref, enc_tile, dec_tile, sems = refs[-8:]
    blocks = []
    chunk = token = 0
    for size in sizes:
        for block in range(size // 64):
            at = slice(block % 2 * 32, (block % 2 + 1) * 32)
            blocks.append((token, chunk + block // 2, chunk + size // 128 + block // 2, at))
            token += 64
        chunk += size // 64
    for token, chunk, _, at in blocks:
        code = spread(sums_ref[chunk, at, :].astype(jnp.float32), rank_ref[token : token + 64, :])
        code_ref[token : token + 64, :] = code.astype(code_ref.dtype)

    steps, cut = enc_tile.shape[:2]
    over_tokens = (((0,), (0,)), ((), ()))
    columns = [slice(step * cut, (step + 1) * cut) for step in range(steps)]
    copies = []
    total = jnp.zeros(bias_ref.shape, jnp.float32)
    for step in range(steps):
        dec = lax.dot_general(
            code_ref[...], read(pieces, cots_at, columns[step]), over_tokens, preferred_element_type=jnp.float32
        )
        dec_tile[step] = dec.astype(dec_tile.dtype)
        copies.append(pltpu.make_async_copy(dec_tile.at[step], dec_ref.at[:, columns[step]], sems.at[0, step]))
        copies[-1].start()
        for token, _, chunk, at in blocks[step * len(blocks) // steps : (step + 1) * len(blocks) // steps]:
            pre = spread(sums_ref[chunk, at, :].astype(jnp.float32), rank_ref[token : token + 64, :])
            pre_ref[token : token + 64, :] = pre.astype(pre_ref.dtype)
            total += jnp.sum(pre, axis=0, keepdims=True)
    bias_ref[...] = total
    for step in range(steps):
        enc = lax.dot_general(
            read(pieces, acts_at, columns[step]), pre_ref[...], over_tokens, preferred_element_type=jnp.float32
        )
        enc_tile[step] = enc.astype(enc_tile.dtype)
        copies.append(pltpu.make_async_copy(enc_tile.at[step], enc_ref.at[columns[step], :], sems.at[1, step]))
        copies[-1].start()
    for copy in copies:
        copy.wait()


def params(mib):
    return pltpu.CompilerParams(vmem_limit_bytes=mib * 1024 * 1024)


def whole():
    return pl.BlockSpec(memory_space=pltpu.VMEM)


def device(x, y, core):
    return (x * 4 + y) * 2 + core


def hop(dx, dy, dcore):
    return [
        (device(x, y, core), device((x + dx) % 2, (y + dy) % 4, (core + dcore) % 2))
        for x in range(2)
        for y in range(4)
        for core in range(2)
    ]


def east(values):
    return lax.ppermute(values, "latent", hop(1, 0, 0))


def up(values):
    return lax.ppermute(values, "latent", hop(0, 1, 0))


def down(values):
    return lax.ppermute(values, "latent", hop(0, -1, 0))


def twin(values):
    return lax.ppermute(values, "latent", hop(0, 0, 1))


ORIGINS = [
    (dx, dy, core)
    for dx, dy in ((0, 0), (1, 0), (0, 3), (0, 1), (1, 3), (1, 1), (0, 2), (1, 2))
    for core in (0, 1)
]


def pack_kernel(outs, *refs):
    sems = refs[-1]
    out_refs = refs[len(refs) - 1 - len(outs) : -1]
    copies = []
    for out_ref, parts in zip(out_refs, outs):
        at = 0
        for n, first, last in parts:
            here = out_ref.at[at : at + last - first]
            copies.append(pltpu.make_async_copy(refs[n].at[first:last], here, sems.at[len(copies)]))
            at += last - first
    for copy in copies:
        copy.start()
    for copy in copies:
        copy.wait()


def pack_all(*groups):
    given, outs = [], []
    for group in groups:
        outs.append([])
        for part in group:
            array, first, last = part if isinstance(part, tuple) else (part, 0, part.shape[0])
            outs[-1].append((len(given), first, last))
            given.append(array)
    width, dtype = given[0].shape[1], given[0].dtype
    totals = [sum(last - first for _, first, last in parts) for parts in outs]
    hbm = pl.BlockSpec(memory_space=pl.ANY)
    return pl.pallas_call(
        functools.partial(pack_kernel, outs),
        in_specs=[hbm] * len(given),
        out_specs=[hbm] * len(outs),
        out_shape=[jax.ShapeDtypeStruct((total, width), dtype) for total in totals],
        scratch_shapes=[pltpu.SemaphoreType.DMA((len(given),))],
        compiler_params=params(2),
        cost_estimate=pl.CostEstimate(flops=0, bytes_accessed=sum(totals) * 8192, transcendentals=0),
        name="pack",
    )(*given)


def pack(*parts):
    return pack_all(parts)[0]


def local(activations, cotangents, enc_weight, dec_weight, enc_bias, active_mask):
    tokens, latents = active_mask.shape
    rows, width = activations.shape[1:]
    blocks = tokens // rows
    half = rows // 2
    f32, bf16 = jnp.float32, jnp.bfloat16
    acts, cots = activations[0], cotangents[0]
    enc, dec = enc_weight[0], dec_weight[0]

    here = lax.axis_index("latent").astype(jnp.int32)
    x, y, core = here // 8, here // 2 % 4, here % 2
    far_x, far_y, far_core = (jnp.array(column, jnp.int32) for column in zip(*ORIGINS))
    order = device((x + far_x) % 2, (y + far_y) % 4, (core + far_core) % 2)
    layer = lax.axis_index("layer").astype(jnp.int32)
    is_code = (layer < 4) | ((layer >= 8) & (layer % 4 < 2))
    block = jnp.where(layer < 8, layer, layer // 2 + layer % 2)
    block = jnp.where(is_code, block, 0)
    place = jnp.stack([block, is_code.astype(jnp.int32)])
    smem = pl.BlockSpec(memory_space=pltpu.SMEM)

    hbm = pl.BlockSpec(memory_space=pl.ANY)
    tie = lax.optimization_barrier
    rank, slot = pl.pallas_call(
        rank_kernel,
        in_specs=[smem, whole()],
        out_specs=[whole(), whole()],
        out_shape=[
            jax.ShapeDtypeStruct((tokens, latents), jnp.int32),
            jax.ShapeDtypeStruct((tokens // 2, 128), jnp.int32),
        ],
        compiler_params=params(12),
        cost_estimate=pl.CostEstimate(flops=3 * 10**9, bytes_accessed=4 * 10**6, transcendentals=0),
        name="ranks",
    )(order, active_mask)
    a_x = east(acts)
    c_low, c_high = up(cots), down(cots)
    a_low, a_high = up(acts), down(acts)
    a_x, cots_later = tie((a_x, cots))
    c_x = east(cots_later)
    c_x_near = east(pack(c_low, c_high))
    sent = pack_all([a_x, (c_low, 0, half)], [a_x, (c_high, half, rows)])
    *sent, a_low, a_high, rank, slot, place = tie((*sent, a_low, a_high, rank, slot, place))
    third_low, third_high = up(sent[0]), down(sent[1])
    sent = pack_all(
        [(third_low, rows, rows + half), (third_high, rows, rows + half)],
        [(a_low, 0, half), (third_low, 0, half)],
        [(a_high, half, rows), (third_high, half, rows)],
    )
    c_x_far, fourth_low, fourth_high = east(sent[0]), up(sent[1]), down(sent[2])

    *first, _ = tie((acts, cots, a_x, c_low, c_high, a_low, a_high, c_x, c_x))
    first = pack(*first)
    second = pack(third_low, third_high, c_x_near)
    sizes = (512, 256, 256)
    acts_at = [
        [[(0, k * rows, (k + 1) * rows)] for k in (0, 2, 5, 6)],
        [[(1, 0, 64)], [(1, 96, 160)]],
        [[(2, 0, 32), (2, 64, 96)], [(2, 32, 64), (2, 96, 128)]],
    ]
    cots_at = [
        [[(0, k * rows, (k + 1) * rows)] for k in (1, 7, 3, 4)],
        [[(1, 192, 256)], [(1, 256, 320)]],
        [[(1, 64, 96), (1, 160, 192)], [(2, 128, 192)]],
    ]

    def with_twins(items, first=0):
        return [(2 * (n - first) + core, *at) for item in items for core in (0, 1) for n, *at in item]

    def terms_of(number, earlier, used):
        size, start, first_piece = sizes[number], sum(sizes[:number]), min(number, 1)
        at = with_twins(acts_at[number], first_piece), with_twins(cots_at[number], first_piece)
        given = sum(array.shape[0] for array in earlier)
        return pl.pallas_call(
            functools.partial(term_kernel, *at, start, len(earlier)),
            in_specs=[whole()] * (len(used) + 3 + len(earlier)),
            out_specs=whole(),
            out_shape=jax.ShapeDtypeStruct((given + size // 64, 64, 128), bf16),
            compiler_params=params(12),
            cost_estimate=pl.CostEstimate(
                flops=4 * size * width * latents, bytes_accessed=4 * size * width, transcendentals=0
            ),
            name=("near", "middle", "far")[number],
        )(*used, enc, dec, slot, *earlier)

    doubled = [first, twin(first)]
    terms = terms_of(0, [], doubled)
    doubled += [second, twin(second)]
    terms = terms_of(1, [terms], doubled[2:])
    *doubled, terms, fourth_low, fourth_high, c_x_far = tie((*doubled, terms, fourth_low, fourth_high, c_x_far))
    last = pack(fourth_low, fourth_high, c_x_far)
    doubled += [last, twin(last)]
    terms = terms_of(2, [terms], doubled[2:])

    mine = lax.all_to_all(terms, "layer", 0, 0)
    sums = pl.pallas_call(
        sum_kernel,
        in_specs=[smem, whole(), whole(), whole()],
        out_specs=whole(),
        out_shape=jax.ShapeDtypeStruct((blocks, rows, 128), bf16),
        compiler_params=params(4),
        name="sums",
    )(place, mine, slot, enc_bias[None, :])
    sums = lax.all_to_all(sums, "layer", 0, 0)

    cut = 256
    all_acts = [at for items in acts_at for at in with_twins(items)]
    all_cots = [at for items in cots_at for at in with_twins(items)]
    enc_grad, dec_grad, bias_grad = pl.pallas_call(
        functools.partial(grad_kernel, all_acts, all_cots, sizes),
        in_specs=[whole()] * (2 + len(doubled)),
        out_specs=[pl.BlockSpec(memory_space=pl.ANY)] * 2 + [whole()],
        out_shape=[
            jax.ShapeDtypeStruct((width, latents), bf16),
            jax.ShapeDtypeStruct((latents, width), bf16),
            jax.ShapeDtypeStruct((1, latents), f32),
        ],
        scratch_shapes=[
            pltpu.VMEM((tokens, latents), bf16),
            pltpu.VMEM((tokens, latents), bf16),
            pltpu.VMEM((width // cut, cut, latents), bf16),
            pltpu.VMEM((width // cut, latents, cut), bf16),
            pltpu.SemaphoreType.DMA((2, width // cut)),
        ],
        compiler_params=params(20),
        name="grads",
    )(sums, rank, *doubled)
    return enc_grad[None], dec_grad[None], bias_grad[0]


def solution(mesh):
    return jax.shard_map(
        local,
        mesh=mesh,
        in_specs=(
            P("layer", "latent", None),
            P("layer", "latent", None),
            P("layer", None, "latent"),
            P("layer", "latent", None),
            P("latent"),
            P(None, "latent"),
        ),
        out_specs=(P("layer", None, "latent"), P("layer", "latent", None), P("latent")),
        check_vma=False,
    )
```

```python
import functools

import jax
import jax.numpy as jnp
from jax import lax
from jax.experimental import pallas as pl
from jax.experimental.pallas import tpu as pltpu
from jax.sharding import PartitionSpec as P

KEEP = 64


def take(values, lanes):
    return jnp.take_along_axis(values, lanes, axis=1, mode="promise_in_bounds")


def tiles_of(array):
    return [array[:, at : at + 128] for at in range(0, array.shape[1], 128)]


def rank_kernel(order_ref, mask_ref, rank_ref, slot_ref):
    latents = mask_ref.shape[1]
    blocks = order_ref.shape[0]
    rows = mask_ref.shape[0] // blocks
    half = rows // 2
    f32, bf16, i32 = jnp.float32, jnp.bfloat16, jnp.int32
    shape = (latents, latents)
    row, column = lax.broadcasted_iota(i32, shape, 0), lax.broadcasted_iota(i32, shape, 1)
    upper = (row <= column).astype(f32).astype(bf16)
    row, column = row[:, :128], column[:, :128]
    ahead = (row < 16 * column).astype(f32).astype(bf16)
    bits = jnp.where(row // 16 == column, jnp.left_shift(1, row % 16), 0).astype(f32).astype(bf16)
    group = 4
    for first in range(0, blocks, group):
        mask = [mask_ref[pl.ds(pl.multiple_of(order_ref[first + k] * rows, rows), rows), :] for k in range(group)]
        mask = jnp.concatenate(mask, axis=0)
        ones = mask.astype(f32).astype(bf16)
        count = jnp.dot(ones, upper, preferred_element_type=f32).astype(i32)
        rank_ref[first * rows : (first + group) * rows, :] = jnp.where(mask > 0, count - 1, -1)
        before = jnp.dot(ones, ahead, preferred_element_type=f32).astype(i32)
        word = jnp.dot(ones, bits, preferred_element_type=f32).astype(i32)
        lane = lax.broadcasted_iota(i32, (group * rows, 128), 1)
        place = lane % KEEP
        segment = jnp.zeros(lane.shape, i32)
        base = jnp.zeros(lane.shape, i32)
        for step in (16, 8, 4, 2, 1):
            seen = take(before, segment + step)
            segment += jnp.where(seen <= place, step, 0)
            base = jnp.where(seen <= place, seen, base)
        word = take(word, segment)
        left = place - base
        at = segment * 16
        for step in (8, 4, 2, 1):
            low = word & ((1 << step) - 1)
            ones = low
            if step > 1:
                ones = (ones & 0x5555) + ((ones >> 1) & 0x5555)
            if step > 2:
                ones = (ones & 0x3333) + ((ones >> 2) & 0x3333)
            if step > 4:
                ones = (ones & 0x0F0F) + ((ones >> 4) & 0x0F0F)
            past = left >= ones
            left = jnp.where(past, left - ones, left)
            word = jnp.where(past, word >> step, low)
            at += jnp.where(past, step, 0)
        for k in range(group):
            one, two = at[k * rows : k * rows + half], at[k * rows + half : (k + 1) * rows]
            to = (first + k) * half
            slot_ref[to : to + half, :] = jnp.where(lane[:half] < KEEP, one, two)


def squeeze(full, slot):
    half = slot.shape[0]
    lane = lax.broadcasted_iota(jnp.int32, (half, 128), 1)
    tile, at = slot // 128, slot % 128
    out = jnp.zeros((half, 128), jnp.float32)
    for number, part in enumerate(tiles_of(full)):
        got = jnp.where(lane < KEEP, take(part[:half], at), take(part[half:], at))
        out = jnp.where(tile == number, got, out)
    return out


def spread(packed, rank):
    half = packed.shape[0]
    parts = []
    for number, place in enumerate(tiles_of(rank)):
        at = jnp.maximum(place, 0)
        got = jnp.concatenate([take(packed, at[:half]), take(packed, at[half:] + KEEP)], axis=0)
        parts.append(jnp.where(place >= 0, got, 0.0))
    return jnp.concatenate(parts, axis=1)


def read(pieces, places, columns=slice(None)):
    return jnp.concatenate([pieces[n][first:last, columns] for n, first, last in places], axis=0)


def term_kernel(acts_at, cots_at, first, earlier, *refs):
    out_ref = refs[-1]
    given = refs[len(refs) - 1 - earlier : -1]
    pieces = refs[: len(refs) - 4 - earlier]
    enc_ref, dec_ref, slot_ref = refs[len(pieces) : len(pieces) + 3]
    chunk = 0
    for ref in given:
        out_ref[chunk : chunk + ref.shape[0]] = ref[...]
        chunk += ref.shape[0]
    pre = jnp.dot(read(pieces, acts_at), enc_ref[...], preferred_element_type=jnp.float32)
    cot = lax.dot_general(
        read(pieces, cots_at), dec_ref[...], (((1,), (1,)), ((), ())), preferred_element_type=jnp.float32
    )
    rows, half = 64, 32
    tokens = pre.shape[0]
    for block in range(tokens // rows):
        slot = slot_ref[first // 2 + block * half : first // 2 + (block + 1) * half, :]
        at = slice(block * rows, (block + 1) * rows)
        to = slice(block % 2 * half, (block % 2 + 1) * half)
        out_ref[chunk + block // 2, to, :] = squeeze(pre[at], slot).astype(out_ref.dtype)
        out_ref[chunk + tokens // 128 + block // 2, to, :] = squeeze(cot[at], slot).astype(out_ref.dtype)


def sum_kernel(place_ref, terms_ref, slot_ref, bias_ref, out_ref):
    total = jnp.sum(terms_ref[...].astype(jnp.float32), axis=0)
    half = total.shape[0]
    bias = jnp.broadcast_to(bias_ref[...], (2 * half, bias_ref.shape[1]))
    slot = slot_ref[pl.ds(pl.multiple_of(place_ref[0] * half, half), half), :]
    total += jnp.where(place_ref[1] > 0, squeeze(bias, slot), 0.0)
    out_ref[...] = jnp.broadcast_to(total.astype(out_ref.dtype)[None], out_ref.shape)


def grad_kernel(acts_at, cots_at, sizes, *refs):
    sums_ref, rank_ref = refs[:2]
    pieces = refs[2:-8]
    enc_ref, dec_ref, bias_ref, code_ref, pre_ref, enc_tile, dec_tile, sems = refs[-8:]
    blocks = []
    chunk = token = 0
    for size in sizes:
        for block in range(size // 64):
            at = slice(block % 2 * 32, (block % 2 + 1) * 32)
            blocks.append((token, chunk + block // 2, chunk + size // 128 + block // 2, at))
            token += 64
        chunk += size // 64
    for token, chunk, _, at in blocks:
        code = spread(sums_ref[chunk, at, :].astype(jnp.float32), rank_ref[token : token + 64, :])
        code_ref[token : token + 64, :] = code.astype(code_ref.dtype)

    steps, cut = enc_tile.shape[:2]
    over_tokens = (((0,), (0,)), ((), ()))
    columns = [slice(step * cut, (step + 1) * cut) for step in range(steps)]
    copies = []
    total = jnp.zeros(bias_ref.shape, jnp.float32)
    for step in range(steps):
        dec = lax.dot_general(
            code_ref[...], read(pieces, cots_at, columns[step]), over_tokens, preferred_element_type=jnp.float32
        )
        dec_tile[step] = dec.astype(dec_tile.dtype)
        copies.append(pltpu.make_async_copy(dec_tile.at[step], dec_ref.at[:, columns[step]], sems.at[0, step]))
        copies[-1].start()
        for token, _, chunk, at in blocks[step * len(blocks) // steps : (step + 1) * len(blocks) // steps]:
            pre = spread(sums_ref[chunk, at, :].astype(jnp.float32), rank_ref[token : token + 64, :])
            pre_ref[token : token + 64, :] = pre.astype(pre_ref.dtype)
            total += jnp.sum(pre, axis=0, keepdims=True)
    bias_ref[...] = total
    for step in range(steps):
        enc = lax.dot_general(
            read(pieces, acts_at, columns[step]), pre_ref[...], over_tokens, preferred_element_type=jnp.float32
        )
        enc_tile[step] = enc.astype(enc_tile.dtype)
        copies.append(pltpu.make_async_copy(enc_tile.at[step], enc_ref.at[columns[step], :], sems.at[1, step]))
        copies[-1].start()
    for copy in copies:
        copy.wait()


def params(mib):
    return pltpu.CompilerParams(vmem_limit_bytes=mib * 1024 * 1024)


def whole():
    return pl.BlockSpec(memory_space=pltpu.VMEM)


def device(x, y, core):
    return (x * 4 + y) * 2 + core


def hop(dx, dy, dcore):
    return [
        (device(x, y, core), device((x + dx) % 2, (y + dy) % 4, (core + dcore) % 2))
        for x in range(2)
        for y in range(4)
        for core in range(2)
    ]


def east(values):
    return lax.ppermute(values, "latent", hop(1, 0, 0))


def up(values):
    return lax.ppermute(values, "latent", hop(0, 1, 0))


def down(values):
    return lax.ppermute(values, "latent", hop(0, -1, 0))


def twin(values):
    return lax.ppermute(values, "latent", hop(0, 0, 1))


ORIGINS = [
    (dx, dy, core)
    for dx, dy in ((0, 0), (1, 0), (0, 3), (0, 1), (1, 3), (1, 1), (0, 2), (1, 2))
    for core in (0, 1)
]


def pack_kernel(outs, *refs):
    sems = refs[-1]
    out_refs = refs[len(refs) - 1 - len(outs) : -1]
    copies = []
    for out_ref, parts in zip(out_refs, outs):
        at = 0
        for n, first, last in parts:
            here = out_ref.at[at : at + last - first]
            copies.append(pltpu.make_async_copy(refs[n].at[first:last], here, sems.at[len(copies)]))
            at += last - first
    for copy in copies:
        copy.start()
    for copy in copies:
        copy.wait()


def pack_all(*groups):
    given, outs = [], []
    for group in groups:
        outs.append([])
        for part in group:
            array, first, last = part if isinstance(part, tuple) else (part, 0, part.shape[0])
            outs[-1].append((len(given), first, last))
            given.append(array)
    width, dtype = given[0].shape[1], given[0].dtype
    totals = [sum(last - first for _, first, last in parts) for parts in outs]
    hbm = pl.BlockSpec(memory_space=pl.ANY)
    return pl.pallas_call(
        functools.partial(pack_kernel, outs),
        in_specs=[hbm] * len(given),
        out_specs=[hbm] * len(outs),
        out_shape=[jax.ShapeDtypeStruct((total, width), dtype) for total in totals],
        scratch_shapes=[pltpu.SemaphoreType.DMA((len(given),))],
        compiler_params=params(2),
        cost_estimate=pl.CostEstimate(flops=0, bytes_accessed=sum(totals) * 8192, transcendentals=0),
        name="pack",
    )(*given)


def pack(*parts):
    return pack_all(parts)[0]


def local(activations, cotangents, enc_weight, dec_weight, enc_bias, active_mask):
    tokens, latents = active_mask.shape
    rows, width = activations.shape[1:]
    blocks = tokens // rows
    half = rows // 2
    f32, bf16 = jnp.float32, jnp.bfloat16
    acts, cots = activations[0], cotangents[0]
    enc, dec = enc_weight[0], dec_weight[0]

    here = lax.axis_index("latent").astype(jnp.int32)
    x, y, core = here // 8, here // 2 % 4, here % 2
    far_x, far_y, far_core = (jnp.array(column, jnp.int32) for column in zip(*ORIGINS))
    order = device((x + far_x) % 2, (y + far_y) % 4, (core + far_core) % 2)
    layer = lax.axis_index("layer").astype(jnp.int32)
    is_code = (layer < 4) | ((layer >= 8) & (layer % 4 < 2))
    block = jnp.where(layer < 8, layer, layer // 2 + layer % 2)
    block = jnp.where(is_code, block, 0)
    place = jnp.stack([block, is_code.astype(jnp.int32)])
    smem = pl.BlockSpec(memory_space=pltpu.SMEM)

    hbm = pl.BlockSpec(memory_space=pl.ANY)
    tie = lax.optimization_barrier
    rank, slot = pl.pallas_call(
        rank_kernel,
        in_specs=[smem, whole()],
        out_specs=[whole(), whole()],
        out_shape=[
            jax.ShapeDtypeStruct((tokens, latents), jnp.int32),
            jax.ShapeDtypeStruct((tokens // 2, 128), jnp.int32),
        ],
        compiler_params=params(12),
        cost_estimate=pl.CostEstimate(flops=3 * 10**9, bytes_accessed=4 * 10**6, transcendentals=0),
        name="ranks",
    )(order, active_mask)
    a_x = east(acts)
    c_low, c_high = up(cots), down(cots)
    a_low, a_high = up(acts), down(acts)
    a_x, cots_later = tie((a_x, cots))
    c_x = east(cots_later)
    c_x_near = east(pack(c_low, c_high))
    sent = pack_all([a_x, (c_low, 0, half)], [a_x, (c_high, half, rows)])
    *sent, a_low, a_high, rank, slot, place = tie((*sent, a_low, a_high, rank, slot, place))
    third_low, third_high = up(sent[0]), down(sent[1])
    sent = pack_all(
        [(third_low, rows, rows + half), (third_high, rows, rows + half)],
        [(a_low, 0, half), (third_low, 0, half)],
        [(a_high, half, rows), (third_high, half, rows)],
    )
    c_x_far, fourth_low, fourth_high = east(sent[0]), up(sent[1]), down(sent[2])

    *first, _ = tie((acts, cots, a_x, c_low, c_high, a_low, a_high, c_x, c_x))
    first = pack(*first)
    second = pack(third_low, third_high, c_x_near)
    sizes = (512, 256, 256)
    acts_at = [
        [[(0, k * rows, (k + 1) * rows)] for k in (0, 2, 5, 6)],
        [[(1, 0, 64)], [(1, 96, 160)]],
        [[(2, 0, 32), (3, 0, 32)], [(2, 32, 64), (3, 32, 64)]],
    ]
    cots_at = [
        [[(0, k * rows, (k + 1) * rows)] for k in (1, 7, 3, 4)],
        [[(1, 192, 256)], [(1, 256, 320)]],
        [[(1, 64, 96), (1, 160, 192)], [(2, 64, 128)]],
    ]

    def with_twins(items, first=0):
        return [(2 * (n - first) + core, *at) for item in items for core in (0, 1) for n, *at in item]

    def terms_of(number, earlier, used):
        size, start, first_piece = sizes[number], sum(sizes[:number]), min(number, 1)
        at = with_twins(acts_at[number], first_piece), with_twins(cots_at[number], first_piece)
        given = sum(array.shape[0] for array in earlier)
        return pl.pallas_call(
            functools.partial(term_kernel, *at, start, len(earlier)),
            in_specs=[whole()] * (len(used) + 3 + len(earlier)),
            out_specs=whole(),
            out_shape=jax.ShapeDtypeStruct((given + size // 64, 64, 128), bf16),
            compiler_params=params(12),
            cost_estimate=pl.CostEstimate(
                flops=4 * size * width * latents, bytes_accessed=4 * size * width, transcendentals=0
            ),
            name=("near", "middle", "far")[number],
        )(*used, enc, dec, slot, *earlier)

    doubled = [first, twin(first)]
    terms = terms_of(0, [], doubled)
    doubled += [second, twin(second)]
    terms = terms_of(1, [terms], doubled[2:])
    *doubled, terms, fourth_low, c_x_far = tie((*doubled, terms, fourth_low, c_x_far))
    last = pack(fourth_low, c_x_far)
    doubled += [last, twin(last), fourth_high, twin(fourth_high)]
    terms = terms_of(2, [terms], doubled[2:])

    mine = lax.all_to_all(terms, "layer", 0, 0)
    sums = pl.pallas_call(
        sum_kernel,
        in_specs=[smem, whole(), whole(), whole()],
        out_specs=whole(),
        out_shape=jax.ShapeDtypeStruct((blocks, rows, 128), bf16),
        compiler_params=params(4),
        name="sums",
    )(place, mine, slot, enc_bias[None, :])
    sums = lax.all_to_all(sums, "layer", 0, 0)

    cut = 256
    all_acts = [at for items in acts_at for at in with_twins(items)]
    all_cots = [at for items in cots_at for at in with_twins(items)]
    enc_grad, dec_grad, bias_grad = pl.pallas_call(
        functools.partial(grad_kernel, all_acts, all_cots, sizes),
        in_specs=[whole()] * (2 + len(doubled)),
        out_specs=[pl.BlockSpec(memory_space=pl.ANY)] * 2 + [whole()],
        out_shape=[
            jax.ShapeDtypeStruct((width, latents), bf16),
            jax.ShapeDtypeStruct((latents, width), bf16),
            jax.ShapeDtypeStruct((1, latents), f32),
        ],
        scratch_shapes=[
            pltpu.VMEM((tokens, latents), bf16),
            pltpu.VMEM((tokens, latents), bf16),
            pltpu.VMEM((width // cut, cut, latents), bf16),
            pltpu.VMEM((width // cut, latents, cut), bf16),
            pltpu.SemaphoreType.DMA((2, width // cut)),
        ],
        compiler_params=params(20),
        name="grads",
    )(sums, rank, *doubled)
    return enc_grad[None], dec_grad[None], bias_grad[0]


def solution(mesh):
    return jax.shard_map(
        local,
        mesh=mesh,
        in_specs=(
            P("layer", "latent", None),
            P("layer", "latent", None),
            P("layer", None, "latent"),
            P("layer", "latent", None),
            P("latent"),
            P(None, "latent"),
        ),
        out_specs=(P("layer", None, "latent"), P("layer", "latent", None), P("latent")),
        check_vma=False,
    )
```
